128 devices in a mesh: sec: 2 (over core), dev: 64 (over y, x, z).
Axes of the slice: x: 4, y: 4, z: 4, core: 2. Of those that a mesh axis runs over, the one named last changes fastest.
Arguments:
- queries: bfloat16 [512, 128, 576], P(('sec', 'dev')), may hold values from -36 to 36
- latent_cache: bfloat16 [512, 2048, 576], P(('sec', 'dev')), may hold values from -6 to 6
- lengths: int32 [512], P(('sec', 'dev')), may hold values from 1 to 2048, 524288 in all
- rows_in: bfloat16 [4096, 3584], P(('sec', 'dev')), may hold values from -6 to 6
- routes: int32 [4096, 8], P(('sec', 'dev')), may hold values from 0 to 63, all different within a row; in each aligned block of 32 rows (0 to 31, 32 to 63, ...) at most 8 rows name the same one
- router_weight: bfloat16 [3584, 64], replicated, may hold values from -0.09375 to 0.09375
- gate_weight: bfloat16 [64, 3584, 1024], P('dev', None, 'sec'), may hold values from -0.09375 to 0.09375
- up_weight: bfloat16 [64, 3584, 1024], P('dev', None, 'sec'), may hold values from -0.09375 to 0.09375
- down_weight: bfloat16 [64, 1024, 3584], P('dev', 'sec'), may hold values from -0.1875 to 0.1875
Outputs:
- latent_out: bfloat16 [512, 128, 512], P(('sec', 'dev'))
- moe_out: bfloat16 [4096, 3584], P(('sec', 'dev'))
The draws below stay inside these ranges and needn't reach their ends.
Inputs may be any that keep to these rules, and one draw needn't show every extreme that they name: `routes`: each row names 8 different experts; among the rows of one device no expert is named more than 8 times, a bound that some block reaches. `lengths`: the largest length is exactly 2048.
All inputs are finite; a program needn't handle non-finite values. No bound on the sum of `lengths` on one device may be relied on, other than what follows from the above.
Results may differ from the reference program's by a relative error of at most 0.012.
Values may be sent and summed in bfloat16 or wider, within the bound.
A program may use at most 128 MiB of HBM per device.

```python
import math
import jax
import jax.numpy as jnp
import numpy as np
from jax import lax

D = 3584
FF = 1024
H = 128
LATENT = 512
ROPE = 64
TOPK = 8
LEN = 2048
ROWS_DEV = 32
EXPERTS = 64
CAP = 8
REQUESTS = 512
TOKENS = 4096
DEVICES = 128


def shared_latents(key):
    drawn = jax.random.normal(key, (REQUESTS, LEN, LATENT + ROPE), jnp.float32)
    return jnp.clip(drawn, -6.0, 6.0)


def draw_latent_cache(key, part):
    latents = shared_latents(key)
    return latents.astype(jnp.bfloat16)


def draw_queries(key, part):
    key = jax.random.fold_in(key, 23)
    drawn = jnp.clip(jax.random.normal(key, (REQUESTS, H, LATENT + ROPE), jnp.float32), -6.0, 6.0)
    return drawn.astype(jnp.bfloat16)


def level_of(stream_key, dims, cuts, smallest, high):
    def one(axis_at, blocks):
        draws = jax.random.uniform(jax.random.fold_in(jax.random.fold_in(stream_key, 6), axis_at), (blocks,), jnp.float32, smallest / len(cuts), high / len(cuts))
        return jnp.repeat(jnp.exp(draws), dims[axis_at] // blocks).reshape((-1,) + (1,) * (len(dims) - axis_at - 1))

    loudness = one(*cuts[0])
    for cut in cuts[1:]:
        loudness = loudness * one(*cut)
    return loudness


def length_profile(count, total, limit, slope):
    portions = [(1 << 20) // math.isqrt(grade ** slope) + 1 for grade in range(2, count + 1)]
    surplus, counts = total - limit - (count - 1), [1] * (count - 1)
    while surplus > 0:
        free = [i for i in range(count - 1) if counts[i] < limit]
        mass, budget = sum([portions[i] for i in free]), surplus
        for i in free:
            addition = min(limit - counts[i], max(1, budget * portions[i] // mass), surplus)
            counts[i] = counts[i] + addition
            surplus = surplus - addition
    return np.array([limit] + counts)


def ragged(own_key, count, total, most, lean):
    if count == 2:
        one = jax.random.randint(own_key, (), max(1, total - most), min(most, total - 1) + 1)
        return jnp.stack([one, total - one])
    tallies = jnp.asarray(length_profile(count, total, most, lean), jnp.int32)
    couples = (count - 1) // 2
    giver, receiver = tallies[1:1 + 2 * couples:2], tallies[2:2 + 2 * couples:2]
    margin = jnp.minimum(giver - 1, most - receiver)
    passed = jax.random.randint(jax.random.fold_in(own_key, 1), (couples,), 0, 1 << 20) % (margin + 1)
    tallies = tallies.at[1:1 + 2 * couples:2].set(giver - passed).at[2:2 + 2 * couples:2].set(receiver + passed)
    return tallies[jax.random.permutation(jax.random.fold_in(own_key, 2), count)]


def routed_block(own_key, own, number, rows, number_of, top, reach, lean):
    order = jax.random.permutation(own_key, number_of)
    crowded, common = load_shares(number_of, rows * top, reach, lean, True), load_shares(number_of, rows * top, reach, lean, False)
    places = jnp.arange(number_of)

    def named(tallies, offset_by):
        used = int((tallies > 0).sum())
        fixed = max(1, used // 4)
        passed = fixed + (places - fixed + offset_by * (used - fixed)) % max(1, number_of - fixed)
        return jnp.zeros((number_of,), jnp.int32).at[order[jnp.where(places < fixed, places, passed)]].set(jnp.asarray(tallies, jnp.int32))

    tallies = jnp.where(number % 4 == 0, named(crowded, number // 4), named(common, number - number // 4 - 1))
    mixed = jax.random.permutation(jax.random.fold_in(own, 3), number_of)
    giver, taker = mixed[0:number_of // 2 * 2:2], mixed[1:number_of // 2 * 2:2]
    margin = jnp.minimum(tallies[giver] - 1, reach - tallies[taker]) // 2
    margin = jnp.where((giver == order[0]) | (taker == order[0]) | (tallies[taker] == 0), 0, jnp.maximum(margin, 0))
    passed = jax.random.randint(jax.random.fold_in(own, 4), (number_of // 2,), 0, 1 << 20) % (margin + 1)
    tallies = tallies.at[giver].add(-passed).at[taker].add(passed)
    items = jnp.searchsorted(jnp.cumsum(tallies), jnp.arange(rows * top), side="right").astype(jnp.int32)
    grid = items.reshape(top, rows).T
    grid = grid[jax.random.permutation(jax.random.fold_in(own, 1), rows)]
    offset_by = jax.random.randint(jax.random.fold_in(own, 2), (rows, 1), 0, top)
    return jnp.take_along_axis(grid, (jnp.arange(top)[None, :] + offset_by) % top, axis=1)


def load_shares(amount, total, reach, slope, full):
    loads = [(1 << 20) // math.isqrt(grade ** slope) + 1 for grade in range(1, amount + 1)]
    largest = reach if full else min(reach, max(-(-total // amount), total * loads[0] // sum(loads)))
    least = 1 if total - largest >= amount - 1 else 0
    counts, surplus = [largest] + [least] * (amount - 1), total - largest - least * (amount - 1)
    while surplus > 0:
        movable = [i for i in range(1, amount) if counts[i] < largest] or [i for i in range(1, amount) if counts[i] < reach]
        mass, left = sum([loads[i] for i in movable]), surplus
        for i in movable:
            more = min(reach - counts[i], max(1, left * loads[i] // mass), surplus)
            counts[i] = counts[i] + more
            surplus = surplus - more
    return np.array(counts)


def noise(rng, shape, scale, most, shards=(), kind=jnp.bfloat16):
    gain = level_of(rng, shape, shards, -0.22, 0.18) if shards else 1.0
    values = jax.random.normal(rng, shape, jnp.float32) * scale * gain
    return jnp.minimum(jnp.maximum(values, -most), most).astype(kind)


def setup_inputs(seed: int = 0) -> dict:
    keys = jax.random.split(jax.random.key(seed), 10)
    queries = draw_queries(jax.random.fold_in(keys[9], 71), 0)
    latent_cache = draw_latent_cache(jax.random.fold_in(keys[9], 71), 0)
    lengths = ragged(keys[2], REQUESTS, REQUESTS * LEN // 2, LEN, 2).astype(jnp.int32)
    rows_in = noise(keys[3], (TOKENS, D), 1.0, 6.0, ((0, 128),))
    routes_keys = jax.random.split(jax.random.fold_in(keys[4], 1), TOKENS // ROWS_DEV)
    routes_turns = jax.random.permutation(jax.random.fold_in(keys[4], 3), TOKENS // ROWS_DEV)
    routes = jax.vmap(lambda own, number: routed_block(jax.random.fold_in(keys[4], 2), own, number, ROWS_DEV, EXPERTS, TOPK, CAP, 2))(routes_keys, routes_turns).reshape((TOKENS, TOPK))
    router_weight = noise(keys[5], (D, EXPERTS), D ** -0.5, 0.09375)
    gate_weight = noise(keys[6], (EXPERTS, D, FF), D ** -0.5, 0.09375, ((0, 64), (2, 2)))
    up_weight = noise(keys[7], (EXPERTS, D, FF), D ** -0.5, 0.09375, ((0, 64), (2, 2)))
    down_weight = noise(keys[8], (EXPERTS, FF, D), FF ** -0.5, 0.1875, ((0, 64), (1, 2)))
    return {"queries": queries, "latent_cache": latent_cache, "lengths": lengths, "rows_in": rows_in, "routes": routes, "router_weight": router_weight, "gate_weight": gate_weight, "up_weight": up_weight, "down_weight": down_weight}


route_scale = 2.5
score_scale = 192.0 ** -0.5


def attend_request(request):
    query_rows, cache_rows, length = request
    scores = jnp.dot(query_rows, cache_rows.T, preferred_element_type=jnp.float32) * score_scale
    position = jnp.arange(LEN, dtype=jnp.int32)
    in_cache = position[None, :] < length
    scores = jnp.where(in_cache, scores, jnp.float32(-1e30))
    row_peak = jnp.max(scores, axis=1, keepdims=True)
    expo = jnp.exp(scores - row_peak)
    weights = (expo / jnp.sum(expo, axis=1, keepdims=True)).astype(jnp.bfloat16)
    return jnp.dot(weights, cache_rows[:, :LATENT], preferred_element_type=jnp.float32).astype(jnp.bfloat16)


def reference(queries, latent_cache, lengths, rows_in, routes, router_weight, gate_weight, up_weight, down_weight):
    latent_out = lax.map(attend_request, (queries, latent_cache, lengths))
    logits = jnp.dot(rows_in, router_weight, preferred_element_type=jnp.float32)
    affinity = jax.nn.sigmoid(logits)
    chosen = jnp.take_along_axis(affinity, routes, axis=1)
    gate_values = (route_scale * chosen / jnp.sum(chosen, axis=1, keepdims=True)).astype(jnp.bfloat16)
    bound = DEVICES * CAP
    half_width = FF // 2

    def one_expert(total, inputs):
        gate_mat, up_mat, down_mat, expert = inputs
        match = routes == expert
        members = jnp.any(match, axis=1)
        weight_row = jnp.sum(jnp.where(match, gate_values.astype(jnp.float32), jnp.float32(0.0)), axis=1)
        member_index = jnp.nonzero(members, size=bound, fill_value=0)[0].astype(jnp.int32)
        valid = jnp.arange(bound, dtype=jnp.int32) < jnp.sum(members.astype(jnp.int32))
        picked = rows_in[member_index]
        gate_part = jnp.dot(picked, gate_mat, preferred_element_type=jnp.float32)
        up_part = jnp.dot(picked, up_mat, preferred_element_type=jnp.float32)
        hidden = (jax.nn.silu(gate_part) * up_part).astype(jnp.bfloat16)
        first = jnp.dot(hidden[:, :half_width], down_mat[:half_width], preferred_element_type=jnp.float32)
        second = jnp.dot(hidden[:, half_width:], down_mat[half_width:], preferred_element_type=jnp.float32)
        first = lax.optimization_barrier(first.astype(jnp.bfloat16)).astype(jnp.float32)
        second = lax.optimization_barrier(second.astype(jnp.bfloat16)).astype(jnp.float32)
        expert_rows = (first + second).astype(jnp.bfloat16)
        scaled = jnp.where(valid, weight_row[member_index], jnp.float32(0.0))
        total = total.at[member_index].add(scaled[:, None] * expert_rows.astype(jnp.float32))
        return total, None

    start = jnp.zeros((TOKENS, D), jnp.float32)
    experts_index = jnp.arange(EXPERTS, dtype=jnp.int32)
    total, unused = lax.scan(one_expert, start, (gate_weight, up_weight, down_weight, experts_index))
    return latent_out, total.astype(jnp.bfloat16)
```

```python
import jax
import jax.numpy as jnp
from jax import lax
from jax.experimental import pallas as pl
from jax.experimental.pallas import tpu as pltpu
from jax.sharding import PartitionSpec as P

MESH = pl.DeviceIdType.MESH
BF, F32 = jnp.bfloat16, jnp.float32
SIDE = 4
STRIDE = {"y": 16, "x": 4, "z": 1}
ROTATIONS = (("x", "y", "z"), ("z", "x", "y"), ("y", "z", "x"))
WIDTHS = (512, 512, 512, 768, 640, 640)
STARTS = tuple(sum(WIDTHS[:i]) for i in range(len(WIDTHS)))
FIRST, SECOND = (0, 1, 2), (3, 4, 5)
PARTS = FIRST + SECOND
EXTRA = 128
TOK, SLOTS, EXPERTS, LATENT = 32, 8, 64, 512
ROUTE_SCALE = 2.5
SCORE_SCALE = 192.0 ** (-0.5)
GATHER_A, GATHER_B, SPREAD, RETURN, SUM_B, SUM_A = range(6)


def block_map(r):
    a_axis, b_axis, c_axis = ROTATIONS[r]
    order = []
    for i in range(64):
        at = {c_axis: i // 16, b_axis: (i // 4) % 4, a_axis: i % 4}
        order.append(at["y"] * 16 + at["x"] * 4 + at["z"])
    return order


BLOCKS = tuple(block_map(r) for r in range(3))


def dot(a, b):
    return jnp.dot(a, b, preferred_element_type=F32)


def dot_nt(a, b):
    return lax.dot_general(a, b, (((1,), (1,)), ((), ())), preferred_element_type=F32)


def iota(shape, dim):
    return lax.broadcasted_iota(jnp.int32, shape, dim)


def body(len_ref, rows_ref, routes_ref, router_ref, q_hbm, kv_hbm, wg_hbm, wu_hbm, wd_hbm, lat_ref, out_ref, *scratch):
    scratch = list(scratch)

    def take(n):
        got = scratch[:n]
        del scratch[:n]
        return got

    wg, wu, wd, acc, qbuf, kvbuf, sbuf = take(7)
    hid, sel, comb = take(3), take(3), take(3)
    pb, tx, rx, back, r2, s2, r1 = (take(6) for _ in range(7))
    send_sem, recv_sem, w_local, w_send, w_recv, kv_sem, q_sem = take(7)

    sec, dev = lax.axis_index("sec"), lax.axis_index("dev")
    pos = {"y": lax.div(dev, 16), "x": lax.rem(lax.div(dev, 4), 4), "z": lax.rem(dev, 4)}

    def peer(axis, k):
        other = lax.rem(pos[axis] + k, SIDE)
        return (sec, dev + (other - pos[axis]) * STRIDE[axis])

    mate = (1 - sec, dev)

    barrier = pltpu.get_barrier_semaphore()
    for axis in ("x", "y", "z"):
        for k in (1, 2, 3):
            pl.semaphore_signal(barrier, inc=1, device_id=peer(axis, k), device_id_type=MESH)
    pl.semaphore_signal(barrier, inc=1, device_id=mate, device_id_type=MESH)

    def kv_copy(i):
        slot = lax.rem(i, 2)
        return pltpu.make_async_copy(kv_hbm.at[i], kvbuf.at[slot], kv_sem.at[slot])

    q_copy = pltpu.make_async_copy(q_hbm, qbuf, q_sem)
    q_copy.start()
    kv_copy(0).start()
    kv_copy(1).start()
    w_pairs = ((wg_hbm, wg), (wu_hbm, wu), (wd_hbm, wd))
    local = [pltpu.make_async_copy(src.at[0], dst.at[sec], w_local.at[i]) for i, (src, dst) in enumerate(w_pairs)]
    for copy in local:
        copy.start()

    affinity = jax.nn.sigmoid(dot(rows_ref[...], router_ref[...]))
    hot = jnp.zeros((TOK, EXPERTS), F32)
    expert = iota((TOK, EXPERTS), 1)
    for k in range(SLOTS):
        hot = hot + jnp.where(routes_ref[:, k : k + 1] == expert, 1.0, 0.0)
    chosen = hot * affinity
    gates = ROUTE_SCALE * chosen / jnp.sum(chosen, axis=1, keepdims=True)
    earlier = jnp.where(iota((TOK, TOK), 1) < iota((TOK, TOK), 0), 1.0, 0.0).astype(BF)
    place = hot * (dot(earlier, hot.astype(BF)) + 1.0)
    info = jnp.concatenate([place, gates], axis=1).astype(BF)

    def axes(p):
        return ROTATIONS[p % 3]

    for p in PARTS:
        a, b, _ = axes(p)
        mine = pb[p].at[pos[b], pos[a]]
        mine[:, : WIDTHS[p]] = rows_ref[:, STARTS[p] : STARTS[p] + WIDTHS[p]]
        if p in FIRST:
            mine[:, WIDTHS[p] :] = info

    def copies(phase, p):
        a, b, c = axes(p)
        made = []
        for k in (1, 2, 3):
            if phase == GATHER_A:
                axis, src = a, pb[p].at[pos[b], pos[a]]
                dst = src
            elif phase == GATHER_B:
                axis, src = b, pb[p].at[pos[b]]
                dst = src
            elif phase == SPREAD:
                axis, src, dst = c, tx[p].at[k - 1], rx[p].at[pos[c]]
            elif phase == RETURN:
                axis, src, dst = c, rx[p].at[lax.rem(pos[c] + k, SIDE)], back[p].at[3 - k]
            elif phase == SUM_B:
                axis, src, dst = b, pb[p].at[lax.rem(pos[b] + k, SIDE), :, :, pl.ds(0, WIDTHS[p])], r2[p].at[3 - k]
            else:
                axis, src, dst = a, s2[p].at[lax.rem(pos[a] + k, SIDE)], r1[p].at[3 - k]
            made.append(
                pltpu.make_async_remote_copy(
                    src_ref=src,
                    dst_ref=dst,
                    send_sem=send_sem.at[phase, p, k - 1],
                    recv_sem=recv_sem.at[phase, p, k - 1],
                    device_id=peer(axis, k),
                    device_id_type=MESH,
                )
            )
        return made

    flights = {}

    def send(phase, p):
        flights[phase, p] = copies(phase, p)
        for copy in flights[phase, p]:
            copy.start()

    def arrived(phase, p):
        for copy in flights[phase, p]:
            copy.wait_recv()

    def sent(phase, p):
        for copy in flights[phase, p]:
            copy.wait_send()

    pl.semaphore_wait(barrier, 10)
    for p in PARTS:
        send(GATHER_A, p)
    swaps = [
        pltpu.make_async_remote_copy(
            src_ref=src.at[0],
            dst_ref=dst.at[sec],
            send_sem=w_send.at[i],
            recv_sem=w_recv.at[i],
            device_id=mate,
            device_id_type=MESH,
        )
        for i, (src, dst) in enumerate(w_pairs)
    ]
    for copy in swaps:
        copy.start()

    def attend(i):
        kv_copy(i).wait()
        keys = kvbuf.at[lax.rem(i, 2)]
        query = qbuf[i]
        filled = len_ref[i]
        peak = jnp.full((128, 1), -1e30, F32)
        for j in range(4):
            s = dot_nt(query, keys[j * 512 : (j + 1) * 512]) * SCORE_SCALE
            s = jnp.where(iota((128, 512), 1) + j * 512 < filled, s, -1e30)
            sbuf[:, j * 512 : (j + 1) * 512] = s
            peak = jnp.maximum(peak, jnp.max(s, axis=1, keepdims=True))
        total = jnp.zeros((128, 1), F32)
        out = jnp.zeros((128, LATENT), F32)
        for j in range(4):
            e = jnp.exp(sbuf[:, j * 512 : (j + 1) * 512] - peak)
            total = total + jnp.sum(e, axis=1, keepdims=True)
            out = out + dot(e.astype(BF), keys[j * 512 : (j + 1) * 512, :LATENT])
        lat_ref[i] = (out / total).astype(BF)

    def lanes_of(r, shift):
        c = ROTATIONS[r][2]
        step = STRIDE[c]
        shape = (256, EXTRA)
        at = lax.rem(pos[c] + lax.div(iota(shape, 0), 64), SIDE)
        wanted = dev - pos[c] * step + at * step + shift
        return jnp.where(iota(shape, 1) == wanted, 1.0, 0.0).astype(BF)

    def info_of(r, half):
        w = WIDTHS[r]
        return pb[r][2 * half : 2 * half + 2, :, :, w : w + EXTRA].reshape(256, EXTRA)

    def build_sel(r):
        shape = (256, 256)
        row, col = iota(shape, 0), iota(shape, 1)
        same = lax.rem(lax.div(row, 8), 8) == lax.div(col, TOK)
        want = (lax.rem(row, 8) + 1).astype(F32)
        pick = lanes_of(r, 0)
        for half in range(2):
            got = dot_nt(pick, info_of(r, half))
            sel[r][half] = jnp.where(same & (got == want), 1.0, 0.0).astype(BF)

    def build_comb(r):
        shape = (256, 256)
        row, col = iota(shape, 0), iota(shape, 1)
        same = lax.rem(lax.div(col, 8), 8) == lax.div(row, TOK)
        want = (lax.rem(col, 8) + 1).astype(F32)
        pick, weigh = lanes_of(r, 0), lanes_of(r, EXPERTS)
        for half in range(2):
            got = dot_nt(info_of(r, half), pick)
            gate = dot_nt(info_of(r, half), weigh)
            comb[r][half] = jnp.where(same & (got == want), gate, 0.0).astype(BF)

    def spread(p):
        w, c = WIDTHS[p], axes(p)[2]
        for half in range(2):
            plane = pb[p][2 * half : 2 * half + 2, :, :, :w].reshape(256, w)
            got = dot(sel[p % 3][half], plane).astype(BF)
            at = slice(64 * half, 64 * half + 64)
            rx[p][pos[c], at] = got[:64]
            for j in range(1, SIDE):
                tx[p][j - 1, at] = got[64 * j : 64 * j + 64]

    def gate_up(p):
        w, r = WIDTHS[p], p % 3
        rows = slice(STARTS[p], STARTS[p] + w)

        @pl.loop(0, 2)
        def _(h):
            for g, weight in enumerate((wg, wu)):
                for n in range(2):
                    cols = slice(256 * n, 256 * n + 256)
                    got = dot(rx[p][...].reshape(512, w), weight[h, rows, cols])
                    for i in range(64):
                        piece = got[8 * i : 8 * i + 8]
                        if p == 0:
                            acc[h, g, BLOCKS[r][i], :, cols] = piece
                        else:
                            acc[h, g, BLOCKS[r][i], :, cols] += piece

    def hidden():
        @pl.loop(0, 2)
        def _(h):
            for n in range(4):
                cols = slice(128 * n, 128 * n + 128)
                pieces = []
                for i in range(64):
                    v = acc[h, 0, i, :, cols]
                    pieces.append(jax.nn.silu(v) * acc[h, 1, i, :, cols])
                for r in range(3):
                    for i in range(0, 64, 2):
                        pair = jnp.concatenate([pieces[BLOCKS[r][i]], pieces[BLOCKS[r][i + 1]]], axis=0)
                        hid[r][h, 8 * i : 8 * i + 16, cols] = pair.astype(BF)

    def down(p):
        w, r = WIDTHS[p], p % 3
        for n in range(0, w, 256):
            wide = min(256, w - n)
            cols = slice(STARTS[p] + n, STARTS[p] + n + wide)
            got = dot(hid[r][0], wd[0, :, cols]) + dot(hid[r][1], wd[1, :, cols])
            rx[p][:, :, n : n + wide] = got.astype(BF).reshape(SIDE, 128, wide)

    def combine(p):
        w, c = WIDTHS[p], axes(p)[2]
        for half in range(2):
            at = slice(64 * half, 64 * half + 64)
            got = jnp.concatenate([rx[p][pos[c], at]] + [back[p][j, at] for j in range(3)], axis=0)
            summed = dot(comb[p % 3][half], got).astype(BF)
            pb[p][2 * half : 2 * half + 2, :, :, :w] = summed.reshape(2, SIDE, TOK, w)

    def sum_b(p):
        w, b = WIDTHS[p], axes(p)[1]
        total = pb[p][pos[b], :, :, :w].astype(F32)
        for j in range(3):
            total = total + r2[p][j].astype(F32)
        s2[p][...] = total.astype(BF)

    def sum_a(p):
        a = axes(p)[0]
        total = s2[p][pos[a]].astype(F32)
        for j in range(3):
            total = total + r1[p][j].astype(F32)
        out_ref[:, STARTS[p] : STARTS[p] + WIDTHS[p]] = total.astype(BF)

    q_copy.wait()
    attend(0)
    kv_copy(2).start()
    for p in PARTS:
        arrived(GATHER_A, p)
        send(GATHER_B, p)
    attend(1)
    kv_copy(3).start()
    attend(2)
    for p in FIRST:
        arrived(GATHER_B, p)
        build_sel(p)
        spread(p)
        send(SPREAD, p)
    for r in range(3):
        build_comb(r)
    attend(3)
    for p in SECOND:
        arrived(GATHER_B, p)
        spread(p)
        send(SPREAD, p)
    for i in range(2):
        local[i].wait()
        swaps[i].wait_recv()
    for p in PARTS:
        arrived(SPREAD, p)
        gate_up(p)
    hidden()
    local[2].wait()
    swaps[2].wait_recv()
    for p in PARTS:
        down(p)
        send(RETURN, p)
    for p in PARTS:
        sent(GATHER_A, p)
        sent(GATHER_B, p)
        arrived(RETURN, p)
        combine(p)
        send(SUM_B, p)
    for p in PARTS:
        arrived(SUM_B, p)
        sum_b(p)
        send(SUM_A, p)
    for p in PARTS:
        arrived(SUM_A, p)
        sum_a(p)
    for copy in swaps:
        copy.wait_send()
    for phase in (SPREAD, RETURN, SUM_B, SUM_A):
        for p in PARTS:
            sent(phase, p)


def per_device(queries, latent_cache, lengths, rows_in, routes, router_weight, gate_weight, up_weight, down_weight):
    width = rows_in.shape[1]
    half = gate_weight.shape[2]
    vmem = pltpu.VMEM

    def each(make):
        return [make(p, WIDTHS[p]) for p in PARTS]

    scratch = [
        vmem((2, width, half), BF),
        vmem((2, width, half), BF),
        vmem((2, half, width), BF),
        vmem((2, 2, 64, 8, half), F32),
        vmem(queries.shape, BF),
        vmem((2,) + latent_cache.shape[1:], BF),
        vmem((queries.shape[1], latent_cache.shape[1]), F32),
    ]
    scratch += [vmem((2, 512, half), BF) for _ in range(3)]
    scratch += [vmem((2, 256, 256), BF) for _ in range(6)]
    scratch += each(lambda p, w: vmem((SIDE, SIDE, TOK, w + (EXTRA if p in FIRST else 0)), BF))
    scratch += each(lambda p, w: vmem((3, 128, w), BF))
    scratch += each(lambda p, w: vmem((SIDE, 128, w), BF))
    scratch += each(lambda p, w: vmem((3, 128, w), BF))
    scratch += each(lambda p, w: vmem((3, SIDE, TOK, w), BF))
    scratch += each(lambda p, w: vmem((SIDE, TOK, w), BF))
    scratch += each(lambda p, w: vmem((3, TOK, w), BF))
    dma = pltpu.SemaphoreType.DMA
    scratch += [dma((6, 6, 3)), dma((6, 6, 3)), dma((3,)), dma((3,)), dma((3,)), dma((2,)), dma]
    whole, stays = pl.BlockSpec(memory_space=pltpu.VMEM), pl.BlockSpec(memory_space=pl.ANY)
    return pl.pallas_call(
        body,
        out_shape=(
            jax.ShapeDtypeStruct(queries.shape[:2] + (LATENT,), BF),
            jax.ShapeDtypeStruct(rows_in.shape, BF),
        ),
        in_specs=[pl.BlockSpec(memory_space=pltpu.SMEM), whole, whole, whole] + [stays] * 5,
        out_specs=(whole, whole),
        scratch_shapes=scratch,
        compiler_params=pltpu.CompilerParams(
            collective_id=0, has_side_effects=True, vmem_limit_bytes=63 << 20
        ),
    )(lengths, rows_in, routes, router_weight, queries, latent_cache, gate_weight, up_weight, down_weight)


def solution(mesh):
    return jax.shard_map(
        per_device,
        mesh=mesh,
        in_specs=(
            P(("sec", "dev"), None, None),
            P(("sec", "dev"), None, None),
            P(("sec", "dev")),
            P(("sec", "dev"), None),
            P(("sec", "dev"), None),
            P(),
            P("dev", None, "sec"),
            P("dev", None, "sec"),
            P("dev", "sec", None),
        ),
        out_specs=(P(("sec", "dev"), None, None), P(("sec", "dev"), None)),
        check_vma=False,
    )
```

```python
import jax
import jax.numpy as jnp
from jax import lax
from jax.experimental import pallas as pl
from jax.experimental.pallas import tpu as pltpu
from jax.sharding import PartitionSpec as P

MESH = pl.DeviceIdType.MESH
BF, F32 = jnp.bfloat16, jnp.float32
SIDE = 4
STRIDE = {"y": 16, "x": 4, "z": 1}
ROTATIONS = (("x", "y", "z"), ("z", "x", "y"), ("y", "z", "x"))
WIDTHS = (512, 512, 512, 768, 640, 640)
STARTS = tuple(sum(WIDTHS[:i]) for i in range(len(WIDTHS)))
PARTS = tuple(range(len(WIDTHS)))
CHUNKS = tuple(PARTS[i : i + 3] for i in range(0, len(WIDTHS), 3))
FIRST = CHUNKS[0]
EXTRA = 128
TOK, SLOTS, EXPERTS, LATENT = 32, 8, 64, 512
ROUTE_SCALE = 2.5
SCORE_SCALE = 192.0 ** (-0.5)
GATHER_A, GATHER_B, RELAY_B, SPREAD, RETURN, FAR_B, SUM_B, SUM_A = range(8)


def block_map(r):
    a_axis, b_axis, c_axis = ROTATIONS[r]
    order = []
    for i in range(64):
        at = {c_axis: i // 16, b_axis: (i // 4) % 4, a_axis: i % 4}
        order.append(at["y"] * 16 + at["x"] * 4 + at["z"])
    return order


BLOCKS = tuple(block_map(r) for r in range(3))


PLACING = (
    tuple(range(0, 64, 2)),
    (),
    tuple(y * 16 + x * 4 + z for x in range(4) for h in range(2) for y in (2 * h, 2 * h + 1) for z in (0, 2)),
)


def dot(a, b):
    return jnp.dot(a, b, preferred_element_type=F32)


def dot_nt(a, b):
    return lax.dot_general(a, b, (((1,), (1,)), ((), ())), preferred_element_type=F32)


def iota(shape, dim):
    return lax.broadcasted_iota(jnp.int32, shape, dim)


def body(len_ref, rows_ref, routes_ref, router_ref, q_hbm, kv_hbm, wg_hbm, wu_hbm, wd_hbm, lat_ref, out_ref, *scratch):
    scratch = list(scratch)

    def take(n):
        got = scratch[:n]
        del scratch[:n]
        return got

    wg, wu, wd, acc, qbuf, kvbuf, sbuf, gathered, hid = take(9)
    sel, comb = take(3), take(3)
    pb, tx, rx, back, far, r2, s2, r1 = (take(len(PARTS)) for _ in range(8))
    send_sem, recv_sem, w_local, w_send, w_recv, kv_sem, q_sem, turn = take(8)

    sec, dev = lax.axis_index("sec"), lax.axis_index("dev")
    pos = {"y": lax.div(dev, 16), "x": lax.rem(lax.div(dev, 4), 4), "z": lax.rem(dev, 4)}

    def peer(axis, k):
        other = lax.rem(pos[axis] + k, SIDE)
        return (sec, dev + (other - pos[axis]) * STRIDE[axis])

    mate = (1 - sec, dev)

    barrier = pltpu.get_barrier_semaphore()
    for axis in ("x", "y", "z"):
        for k in (1, 2, 3):
            pl.semaphore_signal(barrier, inc=1, device_id=peer(axis, k), device_id_type=MESH)
    pl.semaphore_signal(barrier, inc=1, device_id=mate, device_id_type=MESH)

    def kv_copy(i):
        slot = lax.rem(i, 2)
        return pltpu.make_async_copy(kv_hbm.at[i], kvbuf.at[slot], kv_sem.at[slot])

    q_copy = pltpu.make_async_copy(q_hbm, qbuf, q_sem)
    q_copy.start()
    kv_copy(0).start()
    kv_copy(1).start()
    w_pairs = ((wg_hbm, wg), (wu_hbm, wu), (wd_hbm, wd))
    local = [pltpu.make_async_copy(src.at[0], dst.at[sec], w_local.at[i]) for i, (src, dst) in enumerate(w_pairs)]
    for copy in local:
        copy.start()

    affinity = jax.nn.sigmoid(dot_nt(router_ref[...], rows_ref[...]))
    hot = jnp.zeros((EXPERTS, TOK), F32)
    expert = iota((EXPERTS, TOK), 0)
    for k in range(SLOTS):
        hot = hot + jnp.where(routes_ref[k : k + 1, :] == expert, 1.0, 0.0)
    chosen = hot * affinity
    gates = ROUTE_SCALE * chosen / jnp.sum(chosen, axis=0, keepdims=True)
    earlier = jnp.where(iota((TOK, TOK), 0) < iota((TOK, TOK), 1), 1.0, 0.0).astype(BF)
    place = hot * (dot(hot.astype(BF), earlier) + 1.0)
    info = jnp.concatenate([place, gates], axis=0).T.astype(BF)

    def axes(p):
        return ROTATIONS[p % 3]

    for p in PARTS:
        a, b, _ = axes(p)
        mine = pb[p].at[pos[b], pos[a]]
        mine[:, : WIDTHS[p]] = rows_ref[:, STARTS[p] : STARTS[p] + WIDTHS[p]]
        if p in FIRST:
            mine[:, WIDTHS[p] :] = info

    def near(axis, k):
        return lax.rem(pos[axis] + k, SIDE)

    def copies(phase, p):
        a, b, c = axes(p)
        first, second = pl.ds(0, 2), pl.ds(2, 2)
        if phase == GATHER_A:
            src = pb[p].at[pos[b], pos[a]]
            plan = [(a, k, src, src) for k in (1, 2, 3)]
        elif phase == GATHER_B:
            src = pb[p].at[pos[b]]
            plan = [(b, k, src, src) for k in (1, 3)]
        elif phase == RELAY_B:
            up, low = pb[p].at[near(b, 3), first], pb[p].at[near(b, 1), second]
            plan = [(b, 1, up, up), (b, 3, low, low)]
        elif phase == SPREAD:
            plan = [(c, k, tx[p].at[k - 1], rx[p].at[pos[c]]) for k in (1, 2, 3)]
        elif phase == RETURN:
            plan = [(c, k, rx[p].at[near(c, k)], back[p].at[3 - k]) for k in (1, 2, 3)]
        elif phase == FAR_B:
            cols = pl.ds(0, WIDTHS[p])
            plan = [
                (b, 1, pb[p].at[near(b, 2), first, :, cols], far[p].at[0]),
                (b, 3, pb[p].at[near(b, 2), second, :, cols], far[p].at[1]),
            ]
        elif phase == SUM_B:
            cols = pl.ds(0, WIDTHS[p])
            plan = [(b, k, pb[p].at[near(b, k), :, :, cols], r2[p].at[k // 2]) for k in (1, 3)]
        else:
            plan = [(a, k, s2[p].at[near(a, k)], r1[p].at[3 - k]) for k in (1, 2, 3)]
        return [
            pltpu.make_async_remote_copy(
                src_ref=src,
                dst_ref=dst,
                send_sem=send_sem.at[phase, p, i],
                recv_sem=recv_sem.at[phase, p, i],
                device_id=peer(axis, k),
                device_id_type=MESH,
            )
            for i, (axis, k, src, dst) in enumerate(plan)
        ]

    flights = {}

    def send(phase, p):
        flights[phase, p] = copies(phase, p)
        for copy in flights[phase, p]:
            copy.start()

    def arrived(phase, p):
        for copy in flights[phase, p]:
            copy.wait_recv()

    def sent(phase, p):
        for copy in flights[phase, p]:
            copy.wait_send()

    pl.semaphore_wait(barrier, 10)
    for p in PARTS:
        send(GATHER_A, p)
    swaps = [
        pltpu.make_async_remote_copy(
            src_ref=src.at[0],
            dst_ref=dst.at[sec],
            send_sem=w_send.at[i],
            recv_sem=w_recv.at[i],
            device_id=mate,
            device_id_type=MESH,
        )
        for i, (src, dst) in enumerate(w_pairs)
    ]
    for copy in swaps:
        copy.start()

    def attend(i):
        kv_copy(i).wait()
        keys = kvbuf.at[lax.rem(i, 2)]
        query = qbuf[i].T
        filled = len_ref[i]
        peak = jnp.full((128, 1), -1e30, F32)
        for j in range(4):
            s = dot(query, keys[:, j * 512 : (j + 1) * 512]) * SCORE_SCALE
            s = jnp.where(iota((128, 512), 1) + j * 512 < filled, s, -1e30)
            sbuf[:, j * 512 : (j + 1) * 512] = s
            peak = jnp.maximum(peak, jnp.max(s, axis=1, keepdims=True))
        total = jnp.zeros((128, 1), F32)
        out = jnp.zeros((128, LATENT), F32)
        for j in range(4):
            e = jnp.exp(sbuf[:, j * 512 : (j + 1) * 512] - peak)
            total = total + jnp.sum(e, axis=1, keepdims=True)
            out = out + dot_nt(e.astype(BF), keys[:LATENT, j * 512 : (j + 1) * 512])
        lat_ref[i] = (out / total).astype(BF)

    def lanes_of(r, shift):
        c = ROTATIONS[r][2]
        step = STRIDE[c]
        shape = (256, EXTRA)
        at = lax.rem(pos[c] + lax.div(iota(shape, 0), 64), SIDE)
        wanted = dev - pos[c] * step + at * step + shift
        return jnp.where(iota(shape, 1) == wanted, 1.0, 0.0).astype(BF)

    def info_of(r, half):
        w = WIDTHS[r]
        return pb[r][2 * half : 2 * half + 2, :, :, w : w + EXTRA].reshape(256, EXTRA)

    def build_sel(r):
        shape = (256, 256)
        row, col = iota(shape, 0), iota(shape, 1)
        same = lax.rem(lax.div(row, 8), 8) == lax.div(col, TOK)
        want = (lax.rem(row, 8) + 1).astype(F32)
        pick = lanes_of(r, 0)
        for half in range(2):
            got = dot_nt(pick, info_of(r, half))
            sel[r][half] = jnp.where(same & (got == want), 1.0, 0.0).astype(BF)

    def build_comb(r):
        shape = (256, 256)
        row, col = iota(shape, 0), iota(shape, 1)
        same = lax.rem(lax.div(col, 8), 8) == lax.div(row, TOK)
        want = (lax.rem(col, 8) + 1).astype(F32)
        pick, weigh = lanes_of(r, 0), lanes_of(r, EXPERTS)
        for half in range(2):
            got = dot_nt(info_of(r, half), pick)
            gate = dot_nt(info_of(r, half), weigh)
            comb[r][half] = jnp.where(same & (got == want), gate, 0.0).astype(BF)

    def spread(p):
        w, c = WIDTHS[p], axes(p)[2]
        for half in range(2):
            plane = pb[p][2 * half : 2 * half + 2, :, :, :w].reshape(256, w)
            got = dot(sel[p % 3][half], plane).astype(BF)
            at = slice(64 * half, 64 * half + 64)
            rx[p][pos[c], at] = got[:64]
            for j in range(1, SIDE):
                tx[p][j - 1, at] = got[64 * j : 64 * j + 64]

    def place_rows(p):
        w, r = WIDTHS[p], p % 3
        cols = slice(STARTS[p], STARTS[p] + w)
        if r == 1:
            gathered[:, cols] = rx[p][...].reshape(512, w)
            return
        source = {BLOCKS[r][i]: i for i in range(64)}
        loaded = {}

        def piece(block):
            i = source[block]
            if i // 2 not in loaded:
                at = 16 * ((i // 2) % 8)
                loaded[i // 2] = rx[p][i // 16, at : at + 16].astype(F32)
            return loaded[i // 2][8 * (i % 2) : 8 * (i % 2) + 8]

        for block in PLACING[r]:
            pair = jnp.concatenate([piece(block), piece(block + 1)], axis=0)
            gathered[8 * block : 8 * block + 16, cols] = pair.astype(BF)

    def gate_up(chunk):
        begin = STARTS[CHUNKS[chunk][0]]
        rows = slice(begin, begin + sum(WIDTHS[p] for p in CHUNKS[chunk]))

        @pl.loop(0, 2)
        def _(h):
            for n in range(2):
                cols = slice(256 * n, 256 * n + 256)
                parts = []
                for g, weight in enumerate((wg, wu)):
                    got = dot(gathered[:, rows], weight[h, rows, cols])
                    if chunk == 0:
                        acc[h, g, :, cols] = got
                    elif chunk < len(CHUNKS) - 1:
                        acc[h, g, :, cols] += got
                    else:
                        parts.append(got + acc[h, g, :, cols])
                if chunk == len(CHUNKS) - 1:
                    hid[h, :, cols] = (jax.nn.silu(parts[0]) * parts[1]).astype(BF)

    def down(p):
        w, r = WIDTHS[p], p % 3
        for n in range(0, w, 256):
            wide = min(256, w - n)
            cols = slice(STARTS[p] + n, STARTS[p] + n + wide)
            got = dot(hid[0], wd[0, :, cols]) + dot(hid[1], wd[1, :, cols])
            if r == 1:
                rx[p][:, :, n : n + wide] = got.astype(BF).reshape(SIDE, 128, wide)
                continue
            for i in range(0, 64, 2):
                one, two = BLOCKS[r][i], BLOCKS[r][i + 1]
                pair = jnp.concatenate([got[8 * one : 8 * one + 8], got[8 * two : 8 * two + 8]], axis=0)
                at = 8 * (i % 16)
                rx[p][i // 16, at : at + 16, n : n + wide] = pair.astype(BF)

    def combine(p):
        w, c = WIDTHS[p], axes(p)[2]
        for half in range(2):
            at = slice(64 * half, 64 * half + 64)
            got = jnp.concatenate([rx[p][pos[c], at]] + [back[p][j, at] for j in range(3)], axis=0)
            summed = dot(comb[p % 3][half], got).astype(BF)
            pb[p][2 * half : 2 * half + 2, :, :, :w] = summed.reshape(2, SIDE, TOK, w)

    def fold(p):
        w, b = WIDTHS[p], axes(p)[1]
        for k, half in ((1, 0), (3, 1)):
            at = (near(b, k), pl.ds(2 * half, 2), slice(None), pl.ds(0, w))
            pb[p][at] = (pb[p][at].astype(F32) + far[p][half].astype(F32)).astype(BF)

    def sum_b(p):
        w, b = WIDTHS[p], axes(p)[1]
        total = pb[p][pos[b], :, :, :w].astype(F32)
        for j in range(2):
            total = total + r2[p][j].astype(F32)
        s2[p][...] = total.astype(BF)

    def sum_a(p):
        a = axes(p)[0]
        total = s2[p][pos[a]].astype(F32)
        for j in range(3):
            total = total + r1[p][j].astype(F32)
        out_ref[:, STARTS[p] : STARTS[p] + WIDTHS[p]] = total.astype(BF)

    def begin_b(chunk):
        for p in CHUNKS[chunk]:
            arrived(GATHER_A, p)
            send(GATHER_B, p)

    def relay_b(chunk):
        for p in CHUNKS[chunk]:
            arrived(GATHER_B, p)
            send(RELAY_B, p)

    def begin_spread(chunk):
        for p in CHUNKS[chunk]:
            arrived(RELAY_B, p)
            if chunk == 0:
                build_sel(p)
            spread(p)
            send(SPREAD, p)

    def expert_in(chunk):
        for p in CHUNKS[chunk]:
            arrived(SPREAD, p)
            place_rows(p)
        gate_up(chunk)

    def expert_out(chunk):
        for p in CHUNKS[chunk]:
            down(p)
            send(RETURN, p)

    def begin_sum(chunk):
        for p in CHUNKS[chunk]:
            for phase in (GATHER_A, GATHER_B, RELAY_B):
                sent(phase, p)
            arrived(RETURN, p)
            combine(p)
            send(FAR_B, p)

    def fold_b(chunk):
        for p in CHUNKS[chunk]:
            arrived(FAR_B, p)
            fold(p)
            send(SUM_B, p)

    def begin_a(chunk):
        for p in CHUNKS[chunk]:
            arrived(SUM_B, p)
            sum_b(p)
            send(SUM_A, p)

    def finish(chunk):
        for p in CHUNKS[chunk]:
            arrived(SUM_A, p)
            sum_a(p)

    def give_turn():
        @pl.when(sec == 0)
        def _():
            pl.semaphore_signal(turn, inc=1, device_id=mate, device_id_type=MESH)

    def take_turn():
        @pl.when(sec == 1)
        def _():
            pl.semaphore_wait(turn, 1)

    q_copy.wait()
    attend(0)
    kv_copy(2).start()
    begin_b(0)
    attend(1)
    kv_copy(3).start()
    begin_b(1)
    relay_b(0)
    attend(2)
    relay_b(1)
    begin_spread(0)
    for r in range(3):
        build_comb(r)
    begin_spread(1)
    attend(3)
    for i in range(2):
        local[i].wait()
        swaps[i].wait_recv()
    expert_in(0)
    expert_in(1)
    local[2].wait()
    swaps[2].wait_recv()
    expert_out(0)
    expert_out(1)
    begin_sum(0)
    begin_sum(1)
    fold_b(0)
    fold_b(1)
    begin_a(0)
    begin_a(1)
    finish(0)
    finish(1)
    for copy in swaps:
        copy.wait_send()
    for phase in (SPREAD, RETURN, FAR_B, SUM_B, SUM_A):
        for p in PARTS:
            sent(phase, p)


def per_device(queries, latent_cache, lengths, rows_in, routes, router_weight, gate_weight, up_weight, down_weight):
    queries, latent_cache = jnp.swapaxes(queries, 1, 2), jnp.swapaxes(latent_cache, 1, 2)
    routes, router_weight = routes.T, router_weight.T
    width = rows_in.shape[1]
    half = gate_weight.shape[2]
    vmem = pltpu.VMEM

    def each(make):
        return [make(p, WIDTHS[p]) for p in PARTS]

    scratch = [
        vmem((2, width, half), BF),
        vmem((2, width, half), BF),
        vmem((2, half, width), BF),
        vmem((2, 2, 512, half), F32),
        vmem(queries.shape, BF),
        vmem((2,) + latent_cache.shape[1:], BF),
        vmem((queries.shape[2], latent_cache.shape[2]), F32),
    ]
    scratch += [vmem((512, width), BF), vmem((2, 512, half), BF)]
    scratch += [vmem((2, 256, 256), BF) for _ in range(6)]
    scratch += each(lambda p, w: vmem((SIDE, SIDE, TOK, w + (EXTRA if p in FIRST else 0)), BF))
    scratch += each(lambda p, w: vmem((3, 128, w), BF))
    scratch += each(lambda p, w: vmem((SIDE, 128, w), BF))
    scratch += each(lambda p, w: vmem((3, 128, w), BF))
    scratch += each(lambda p, w: vmem((2, 2, TOK, w), BF))
    scratch += each(lambda p, w: vmem((2, SIDE, TOK, w), BF))
    scratch += each(lambda p, w: vmem((SIDE, TOK, w), BF))
    scratch += each(lambda p, w: vmem((3, TOK, w), BF))
    dma = pltpu.SemaphoreType.DMA
    scratch += [dma((8, len(PARTS), 3)), dma((8, len(PARTS), 3)), dma((3,)), dma((3,)), dma((3,)), dma((2,)), dma]
    scratch += [pltpu.SemaphoreType.REGULAR]
    whole, stays = pl.BlockSpec(memory_space=pltpu.VMEM), pl.BlockSpec(memory_space=pl.ANY)
    return pl.pallas_call(
        body,
        out_shape=(
            jax.ShapeDtypeStruct((queries.shape[0], queries.shape[2], LATENT), BF),
            jax.ShapeDtypeStruct(rows_in.shape, BF),
        ),
        in_specs=[pl.BlockSpec(memory_space=pltpu.SMEM), whole, whole, whole] + [stays] * 5,
        out_specs=(whole, whole),
        scratch_shapes=scratch,
        compiler_params=pltpu.CompilerParams(
            collective_id=0, has_side_effects=True, vmem_limit_bytes=63 << 20
        ),
    )(lengths, rows_in, routes, router_weight, queries, latent_cache, gate_weight, up_weight, down_weight)


def solution(mesh):
    return jax.shard_map(
        per_device,
        mesh=mesh,
        in_specs=(
            P(("sec", "dev"), None, None),
            P(("sec", "dev"), None, None),
            P(("sec", "dev")),
            P(("sec", "dev"), None),
            P(("sec", "dev"), None),
            P(),
            P("dev", None, "sec"),
            P("dev", None, "sec"),
            P("dev", "sec", None),
        ),
        out_specs=(P(("sec", "dev"), None, None), P(("sec", "dev"), None)),
        check_vma=False,
    )
```

```python
import jax
import jax.numpy as jnp
from jax import lax
from jax.experimental import pallas as pl
from jax.experimental.pallas import tpu as pltpu
from jax.sharding import PartitionSpec as P

MESH = pl.DeviceIdType.MESH
BF, F32 = jnp.bfloat16, jnp.float32
SIDE = 4
STRIDE = {"y": 16, "x": 4, "z": 1}
ROTATIONS = (("x", "y", "z"), ("z", "x", "y"), ("y", "z", "x"))
WIDTHS = (512, 512, 512, 512, 384, 384, 256, 256, 256)
STARTS = tuple(sum(WIDTHS[:i]) for i in range(len(WIDTHS)))
PARTS = tuple(range(len(WIDTHS)))
CHUNKS = tuple(PARTS[i : i + 3] for i in range(0, len(WIDTHS), 3))
FIRST = CHUNKS[0]
EXTRA = 128
TOK, SLOTS, EXPERTS, LATENT = 32, 8, 64, 512
ROUTE_SCALE = 2.5
SCORE_SCALE = 192.0 ** (-0.5)
GATHER_A, GATHER_B, RELAY_B, SPREAD, RETURN, FAR_B, SUM_B, SUM_A = range(8)


def block_map(r):
    a_axis, b_axis, c_axis = ROTATIONS[r]
    order = []
    for i in range(64):
        at = {c_axis: i // 16, b_axis: (i // 4) % 4, a_axis: i % 4}
        order.append(at["y"] * 16 + at["x"] * 4 + at["z"])
    return order


BLOCKS = tuple(block_map(r) for r in range(3))


PLACING = (
    tuple(range(0, 64, 2)),
    (),
    tuple(y * 16 + x * 4 + z for x in range(4) for h in range(2) for y in (2 * h, 2 * h + 1) for z in (0, 2)),
)


def dot(a, b):
    return jnp.dot(a, b, preferred_element_type=F32)


def dot_nt(a, b):
    return lax.dot_general(a, b, (((1,), (1,)), ((), ())), preferred_element_type=F32)


def iota(shape, dim):
    return lax.broadcasted_iota(jnp.int32, shape, dim)


def body(len_ref, rows_hbm, routes_hbm, router_hbm, q_hbm, kv_hbm, wg_hbm, wu_hbm, wd_hbm, lat_ref, out_ref, *scratch):
    scratch = list(scratch)

    def take(n):
        got = scratch[:n]
        del scratch[:n]
        return got

    rows_ref, routes_ref, router_ref = take(3)
    wg, wu, wd, acc, qbuf, kvbuf, sbuf, gathered, hid = take(9)
    sel, comb = take(3), take(3)
    pb, tx, rx, back, far, r2, s2, r1 = (take(len(PARTS)) for _ in range(8))
    send_sem, recv_sem, w_local, w_send, w_recv, kv_sem, q_sem, in_sem, info_send, info_recv = take(10)

    sec, dev = lax.axis_index("sec"), lax.axis_index("dev")
    pos = {"y": lax.div(dev, 16), "x": lax.rem(lax.div(dev, 4), 4), "z": lax.rem(dev, 4)}

    def peer(axis, k):
        other = lax.rem(pos[axis] + k, SIDE)
        return (sec, dev + (other - pos[axis]) * STRIDE[axis])

    mate = (1 - sec, dev)

    barrier = pltpu.get_barrier_semaphore()
    for axis in ("x", "y", "z"):
        for k in (1, 2, 3):
            pl.semaphore_signal(barrier, inc=1, device_id=peer(axis, k), device_id_type=MESH)
    pl.semaphore_signal(barrier, inc=1, device_id=mate, device_id_type=MESH)

    def kv_copy(i):
        slot = lax.rem(i, 2)
        return pltpu.make_async_copy(kv_hbm.at[i], kvbuf.at[slot], kv_sem.at[slot])

    small = [
        pltpu.make_async_copy(src, dst, in_sem.at[i])
        for i, (src, dst) in enumerate(((rows_hbm, rows_ref), (router_hbm, router_ref), (routes_hbm, routes_ref)))
    ]
    for copy in small:
        copy.start()
    q_copy = pltpu.make_async_copy(q_hbm, qbuf, q_sem)
    q_copy.start()
    kv_copy(0).start()
    w_pairs = ((wg_hbm, wg), (wu_hbm, wu), (wd_hbm, wd))
    local = [pltpu.make_async_copy(src.at[0], dst.at[sec], w_local.at[i]) for i, (src, dst) in enumerate(w_pairs)]

    def axes(p):
        return ROTATIONS[p % 3]

    def near(axis, k):
        return lax.rem(pos[axis] + k, SIDE)

    def copies(phase, p):
        a, b, c = axes(p)
        first, second = pl.ds(0, 2), pl.ds(2, 2)
        if phase == GATHER_A:
            src = pb[p].at[pos[b], pos[a], :, pl.ds(0, WIDTHS[p])]
            plan = [(a, k, src, src) for k in (2, 1, 3)]
        elif phase == GATHER_B:
            src = pb[p].at[pos[b]]
            plan = [(b, k, src, src) for k in (1, 3)]
        elif phase == RELAY_B:
            up, low = pb[p].at[near(b, 3), first], pb[p].at[near(b, 1), second]
            plan = [(b, 1, up, up), (b, 3, low, low)]
        elif phase == SPREAD:
            plan = [(c, k, tx[p].at[k - 1], rx[p].at[pos[c]]) for k in (2, 1, 3)]
        elif phase == RETURN:
            plan = [(c, k, rx[p].at[near(c, k)], back[p].at[3 - k]) for k in (2, 1, 3)]
        elif phase == FAR_B:
            cols = pl.ds(0, WIDTHS[p])
            plan = [
                (b, 1, pb[p].at[near(b, 2), first, :, cols], far[p].at[0]),
                (b, 3, pb[p].at[near(b, 2), second, :, cols], far[p].at[1]),
            ]
        elif phase == SUM_B:
            cols = pl.ds(0, WIDTHS[p])
            plan = [(b, k, pb[p].at[near(b, k), :, :, cols], r2[p].at[k // 2]) for k in (1, 3)]
        else:
            plan = [(a, k, s2[p].at[near(a, k)], r1[p].at[3 - k]) for k in (2, 1, 3)]
        return [
            pltpu.make_async_remote_copy(
                src_ref=src,
                dst_ref=dst,
                send_sem=send_sem.at[phase, p, i],
                recv_sem=recv_sem.at[phase, p, i],
                device_id=peer(axis, k),
                device_id_type=MESH,
            )
            for i, (axis, k, src, dst) in enumerate(plan)
        ]

    flights = {}

    def send(phase, p):
        flights[phase, p] = copies(phase, p)
        for copy in flights[phase, p]:
            copy.start()

    def arrived(phase, p):
        for copy in flights[phase, p]:
            copy.wait_recv()

    def sent(phase, p):
        for copy in flights[phase, p]:
            copy.wait_send()

    small[0].wait()
    for p in PARTS:
        a, b, _ = axes(p)
        pb[p][pos[b], pos[a], :, : WIDTHS[p]] = rows_ref[:, STARTS[p] : STARTS[p] + WIDTHS[p]]
    pl.semaphore_wait(barrier, 10)
    for p in FIRST:
        send(GATHER_A, p)
    for copy in small[1:]:
        copy.wait()

    affinity = jax.nn.sigmoid(dot_nt(router_ref[...], rows_ref[...]))
    hot = jnp.zeros((EXPERTS, TOK), F32)
    expert = iota((EXPERTS, TOK), 0)
    for k in range(SLOTS):
        hot = hot + jnp.where(routes_ref[k : k + 1, :] == expert, 1.0, 0.0)
    chosen = hot * affinity
    gates = ROUTE_SCALE * chosen / jnp.sum(chosen, axis=0, keepdims=True)
    earlier = jnp.where(iota((TOK, TOK), 0) < iota((TOK, TOK), 1), 1.0, 0.0).astype(BF)
    place = hot * (dot(hot.astype(BF), earlier) + 1.0)
    info = jnp.concatenate([place, gates], axis=0).T.astype(BF)

    info_flights = []
    for r in FIRST:
        a, b, _ = axes(r)
        mine = pb[r].at[pos[b], pos[a], :, pl.ds(WIDTHS[r], EXTRA)]
        mine[...] = info
        for k in (2, 1, 3):
            info_flights.append(
                pltpu.make_async_remote_copy(
                    src_ref=mine,
                    dst_ref=mine,
                    send_sem=info_send.at[r, k - 1],
                    recv_sem=info_recv.at[r, k - 1],
                    device_id=peer(a, k),
                    device_id_type=MESH,
                )
            )
    for copy in info_flights:
        copy.start()
    for p in PARTS[3:]:
        send(GATHER_A, p)
    kv_copy(1).start()
    for copy in local:
        copy.start()
    swaps = [
        pltpu.make_async_remote_copy(
            src_ref=src.at[0],
            dst_ref=dst.at[sec],
            send_sem=w_send.at[i],
            recv_sem=w_recv.at[i],
            device_id=mate,
            device_id_type=MESH,
        )
        for i, (src, dst) in enumerate(w_pairs)
    ]
    for copy in swaps:
        copy.start()


    def attend(i):
        kv_copy(i).wait()
        keys = kvbuf.at[lax.rem(i, 2)]
        query = qbuf[i].T
        filled = len_ref[i]
        peak = jnp.full((128, 1), -1e30, F32)
        for j in range(4):
            s = dot(query, keys[:, j * 512 : (j + 1) * 512]) * SCORE_SCALE
            s = jnp.where(iota((128, 512), 1) + j * 512 < filled, s, -1e30)
            sbuf[:, j * 512 : (j + 1) * 512] = s
            peak = jnp.maximum(peak, jnp.max(s, axis=1, keepdims=True))
        total = jnp.zeros((128, 1), F32)
        out = jnp.zeros((128, LATENT), F32)
        for j in range(4):
            e = jnp.exp(sbuf[:, j * 512 : (j + 1) * 512] - peak)
            total = total + jnp.sum(e, axis=1, keepdims=True)
            out = out + dot_nt(e.astype(BF), keys[:LATENT, j * 512 : (j + 1) * 512])
        lat_ref[i] = (out / total).astype(BF)

    def lanes_of(r, shift):
        c = ROTATIONS[r][2]
        step = STRIDE[c]
        shape = (256, EXTRA)
        at = lax.rem(pos[c] + lax.div(iota(shape, 0), 64), SIDE)
        wanted = dev - pos[c] * step + at * step + shift
        return jnp.where(iota(shape, 1) == wanted, 1.0, 0.0).astype(BF)

    def info_of(r, half):
        w = WIDTHS[r]
        return pb[r][2 * half : 2 * half + 2, :, :, w : w + EXTRA].reshape(256, EXTRA)

    def build_sel(r):
        shape = (256, 256)
        row, col = iota(shape, 0), iota(shape, 1)
        same = lax.rem(lax.div(row, 8), 8) == lax.div(col, TOK)
        want = (lax.rem(row, 8) + 1).astype(F32)
        pick = lanes_of(r, 0)
        for half in range(2):
            got = dot_nt(pick, info_of(r, half))
            sel[r][half] = jnp.where(same & (got == want), 1.0, 0.0).astype(BF)

    def build_comb(r):
        shape = (256, 256)
        row, col = iota(shape, 0), iota(shape, 1)
        same = lax.rem(lax.div(col, 8), 8) == lax.div(row, TOK)
        want = (lax.rem(col, 8) + 1).astype(F32)
        pick, weigh = lanes_of(r, 0), lanes_of(r, EXPERTS)
        for half in range(2):
            got = dot_nt(info_of(r, half), pick)
            gate = dot_nt(info_of(r, half), weigh)
            comb[r][half] = jnp.where(same & (got == want), gate, 0.0).astype(BF)

    def spread(p):
        w, c = WIDTHS[p], axes(p)[2]
        for half in range(2):
            plane = pb[p][2 * half : 2 * half + 2, :, :, :w].reshape(256, w)
            got = dot(sel[p % 3][half], plane).astype(BF)
            at = slice(64 * half, 64 * half + 64)
            rx[p][pos[c], at] = got[:64]
            for j in range(1, SIDE):
                tx[p][j - 1, at] = got[64 * j : 64 * j + 64]

    def place_rows(p):
        w, r = WIDTHS[p], p % 3
        cols = slice(STARTS[p], STARTS[p] + w)
        if r == 1:
            gathered[:, cols] = rx[p][...].reshape(512, w)
            return
        source = {BLOCKS[r][i]: i for i in range(64)}
        loaded = {}

        def piece(block):
            i = source[block]
            if i // 2 not in loaded:
                at = 16 * ((i // 2) % 8)
                loaded[i // 2] = rx[p][i // 16, at : at + 16].astype(F32)
            return loaded[i // 2][8 * (i % 2) : 8 * (i % 2) + 8]

        for block in PLACING[r]:
            pair = jnp.concatenate([piece(block), piece(block + 1)], axis=0)
            gathered[8 * block : 8 * block + 16, cols] = pair.astype(BF)

    def gate_up(chunk):
        begin = STARTS[CHUNKS[chunk][0]]
        rows = slice(begin, begin + sum(WIDTHS[p] for p in CHUNKS[chunk]))

        @pl.loop(0, 2)
        def _(h):
            for n in range(2):
                cols = slice(256 * n, 256 * n + 256)
                parts = []
                for g, weight in enumerate((wg, wu)):
                    got = dot(gathered[:, rows], weight[h, rows, cols])
                    if chunk == 0:
                        acc[h, g, :, cols] = got
                    elif chunk < len(CHUNKS) - 1:
                        acc[h, g, :, cols] += got
                    else:
                        parts.append(got + acc[h, g, :, cols])
                if chunk == len(CHUNKS) - 1:
                    hid[h, :, cols] = (jax.nn.silu(parts[0]) * parts[1]).astype(BF)

    def down(p):
        w, r = WIDTHS[p], p % 3
        for n in range(0, w, 256):
            wide = min(256, w - n)
            cols = slice(STARTS[p] + n, STARTS[p] + n + wide)
            got = dot(hid[0], wd[0, :, cols]) + dot(hid[1], wd[1, :, cols])
            if r == 1:
                rx[p][:, :, n : n + wide] = got.astype(BF).reshape(SIDE, 128, wide)
                continue
            for i in range(0, 64, 2):
                one, two = BLOCKS[r][i], BLOCKS[r][i + 1]
                pair = jnp.concatenate([got[8 * one : 8 * one + 8], got[8 * two : 8 * two + 8]], axis=0)
                at = 8 * (i % 16)
                rx[p][i // 16, at : at + 16, n : n + wide] = pair.astype(BF)

    def combine(p):
        w, c = WIDTHS[p], axes(p)[2]
        for half in range(2):
            at = slice(64 * half, 64 * half + 64)
            got = jnp.concatenate([rx[p][pos[c], at]] + [back[p][j, at] for j in range(3)], axis=0)
            summed = dot(comb[p % 3][half], got).astype(BF)
            pb[p][2 * half : 2 * half + 2, :, :, :w] = summed.reshape(2, SIDE, TOK, w)

    def fold(p):
        w, b = WIDTHS[p], axes(p)[1]
        for k, half in ((1, 0), (3, 1)):
            at = (near(b, k), pl.ds(2 * half, 2), slice(None), pl.ds(0, w))
            pb[p][at] = (pb[p][at].astype(F32) + far[p][half].astype(F32)).astype(BF)

    def sum_b(p):
        w, b = WIDTHS[p], axes(p)[1]
        total = pb[p][pos[b], :, :, :w].astype(F32)
        for j in range(2):
            total = total + r2[p][j].astype(F32)
        s2[p][...] = total.astype(BF)

    def sum_a(p):
        a = axes(p)[0]
        total = s2[p][pos[a]].astype(F32)
        for j in range(3):
            total = total + r1[p][j].astype(F32)
        out_ref[:, STARTS[p] : STARTS[p] + WIDTHS[p]] = total.astype(BF)

    def begin_b(chunk):
        for p in CHUNKS[chunk]:
            arrived(GATHER_A, p)
            if chunk == 0:
                for copy in info_flights[3 * p : 3 * p + 3]:
                    copy.wait_recv()
            send(GATHER_B, p)

    def relay_b(chunk):
        for p in CHUNKS[chunk]:
            arrived(GATHER_B, p)
            send(RELAY_B, p)

    def begin_spread(chunk):
        for p in CHUNKS[chunk]:
            arrived(RELAY_B, p)
            if chunk == 0:
                build_sel(p)
            spread(p)
            send(SPREAD, p)

    def expert_in(chunk):
        for p in CHUNKS[chunk]:
            arrived(SPREAD, p)
            place_rows(p)
        gate_up(chunk)

    def expert_out(chunk):
        for p in CHUNKS[chunk]:
            down(p)
            send(RETURN, p)

    def begin_sum(chunk):
        for p in CHUNKS[chunk]:
            for phase in (GATHER_A, GATHER_B, RELAY_B):
                sent(phase, p)
            if p in FIRST:
                for copy in info_flights[3 * p : 3 * p + 3]:
                    copy.wait_send()
            arrived(RETURN, p)
            combine(p)
            send(FAR_B, p)

    def fold_b(chunk):
        for p in CHUNKS[chunk]:
            arrived(FAR_B, p)
            fold(p)
            send(SUM_B, p)

    def begin_a(chunk):
        for p in CHUNKS[chunk]:
            arrived(SUM_B, p)
            sum_b(p)
            send(SUM_A, p)

    def finish(chunk):
        for p in CHUNKS[chunk]:
            arrived(SUM_A, p)
            sum_a(p)

    q_copy.wait()
    attend(0)
    kv_copy(2).start()
    begin_b(0)
    begin_b(1)
    begin_b(2)
    attend(1)
    kv_copy(3).start()
    attend(2)
    relay_b(0)
    relay_b(1)
    relay_b(2)
    attend(3)
    begin_spread(0)
    begin_spread(1)
    begin_spread(2)
    for r in range(3):
        build_comb(r)
    for i in range(2):
        local[i].wait()
        swaps[i].wait_recv()
    expert_in(0)
    expert_in(1)
    expert_in(2)
    local[2].wait()
    swaps[2].wait_recv()
    expert_out(0)
    expert_out(1)
    expert_out(2)
    begin_sum(0)
    begin_sum(1)
    begin_sum(2)
    fold_b(0)
    fold_b(1)
    fold_b(2)
    begin_a(0)
    begin_a(1)
    begin_a(2)
    finish(0)
    finish(1)
    finish(2)
    for copy in swaps:
        copy.wait_send()
    for phase in (SPREAD, RETURN, FAR_B, SUM_B, SUM_A):
        for p in PARTS:
            sent(phase, p)


def hand_over(lat_in, moe_in, lat_out, moe_out):
    lat_out[...] = lat_in[...]
    moe_out[...] = moe_in[...]


def per_device(queries, latent_cache, lengths, rows_in, routes, router_weight, gate_weight, up_weight, down_weight):
    queries, latent_cache = jnp.swapaxes(queries, 1, 2), jnp.swapaxes(latent_cache, 1, 2)
    routes, router_weight = routes.T, router_weight.T
    width = rows_in.shape[1]
    half = gate_weight.shape[2]
    vmem = pltpu.VMEM

    def each(make):
        return [make(p, WIDTHS[p]) for p in PARTS]

    scratch = [
        vmem(rows_in.shape, BF),
        vmem(routes.shape, jnp.int32),
        vmem(router_weight.shape, BF),
        vmem((2, width, half), BF),
        vmem((2, width, half), BF),
        vmem((2, half, width), BF),
        vmem((2, 2, 512, half), F32),
        vmem(queries.shape, BF),
        vmem((2,) + latent_cache.shape[1:], BF),
        vmem((queries.shape[2], latent_cache.shape[2]), F32),
    ]
    scratch += [vmem((512, width), BF), vmem((2, 512, half), BF)]
    scratch += [vmem((2, 256, 256), BF) for _ in range(6)]
    scratch += each(lambda p, w: vmem((SIDE, SIDE, TOK, w + (EXTRA if p in FIRST else 0)), BF))
    scratch += each(lambda p, w: vmem((3, 128, w), BF))
    scratch += each(lambda p, w: vmem((SIDE, 128, w), BF))
    scratch += each(lambda p, w: vmem((3, 128, w), BF))
    scratch += each(lambda p, w: vmem((2, 2, TOK, w), BF))
    scratch += each(lambda p, w: vmem((2, SIDE, TOK, w), BF))
    scratch += each(lambda p, w: vmem((SIDE, TOK, w), BF))
    scratch += each(lambda p, w: vmem((3, TOK, w), BF))
    dma = pltpu.SemaphoreType.DMA
    scratch += [dma((8, len(PARTS), 3)), dma((8, len(PARTS), 3)), dma((3,)), dma((3,)), dma((3,)), dma((2,)), dma]
    scratch += [dma((3,)), dma((3, 3)), dma((3, 3))]
    whole, stays = pl.BlockSpec(memory_space=pltpu.VMEM), pl.BlockSpec(memory_space=pl.ANY)
    results = pl.pallas_call(
        body,
        out_shape=(
            jax.ShapeDtypeStruct((queries.shape[0], queries.shape[2], LATENT), BF),
            jax.ShapeDtypeStruct(rows_in.shape, BF),
        ),
        in_specs=[pl.BlockSpec(memory_space=pltpu.SMEM)] + [stays] * 8,
        out_specs=(whole, whole),
        scratch_shapes=scratch,
        compiler_params=pltpu.CompilerParams(
            collective_id=0, has_side_effects=True, vmem_limit_bytes=63 << 20
        ),
    )(lengths, rows_in, routes, router_weight, queries, latent_cache, gate_weight, up_weight, down_weight)
    return pl.pallas_call(
        hand_over,
        out_shape=[jax.ShapeDtypeStruct(x.shape, x.dtype) for x in results],
        in_specs=[whole, whole],
        out_specs=[whole, whole],
        compiler_params=pltpu.CompilerParams(vmem_limit_bytes=63 << 20),
    )(*results)


def solution(mesh):
    return jax.shard_map(
        per_device,
        mesh=mesh,
        in_specs=(
            P(("sec", "dev"), None, None),
            P(("sec", "dev"), None, None),
            P(("sec", "dev")),
            P(("sec", "dev"), None),
            P(("sec", "dev"), None),
            P(),
            P("dev", None, "sec"),
            P("dev", None, "sec"),
            P("dev", "sec", None),
        ),
        out_specs=(P(("sec", "dev"), None, None), P(("sec", "dev"), None)),
        check_vma=False,
    )
```

```python
import jax
import jax.numpy as jnp
from jax import lax
from jax.experimental import pallas as pl
from jax.experimental.pallas import tpu as pltpu
from jax.sharding import PartitionSpec as P

MESH = pl.DeviceIdType.MESH
BF, F32 = jnp.bfloat16, jnp.float32
SIDE = 4
STRIDE = {"y": 16, "x": 4, "z": 1}
ROTATIONS = (("x", "y", "z"), ("z", "x", "y"), ("y", "z", "x"))
WIDTHS = (512, 512, 512, 512, 384, 384, 256, 256, 256)
STARTS = tuple(sum(WIDTHS[:i]) for i in range(len(WIDTHS)))
PARTS = tuple(range(len(WIDTHS)))
CHUNKS = tuple(PARTS[i : i + 3] for i in range(0, len(WIDTHS), 3))
FIRST = CHUNKS[0]
EXTRA = 128
TOK, SLOTS, EXPERTS, LATENT = 32, 8, 64, 512
ROUTE_SCALE = 2.5
SCORE_SCALE = 192.0 ** (-0.5)
GATHER_A, GATHER_B, RELAY_B, SPREAD, RETURN, FAR_B, SUM_B, SUM_A = range(8)


def block_map(r):
    a_axis, b_axis, c_axis = ROTATIONS[r]
    order = []
    for i in range(64):
        at = {c_axis: i // 16, b_axis: (i // 4) % 4, a_axis: i % 4}
        order.append(at["y"] * 16 + at["x"] * 4 + at["z"])
    return order


BLOCKS = tuple(block_map(r) for r in range(3))


PLACING = (
    tuple(range(0, 64, 2)),
    (),
    tuple(y * 16 + x * 4 + z for x in range(4) for h in range(2) for y in (2 * h, 2 * h + 1) for z in (0, 2)),
)


def dot(a, b):
    return jnp.dot(a, b, preferred_element_type=F32)


def dot_nt(a, b):
    return lax.dot_general(a, b, (((1,), (1,)), ((), ())), preferred_element_type=F32)


def iota(shape, dim):
    return lax.broadcasted_iota(jnp.int32, shape, dim)


def body(len_ref, rows_hbm, routes_hbm, router_hbm, q_hbm, kv_hbm, wg_hbm, wu_hbm, wd_hbm, lat_ref, out_ref, *scratch):
    scratch = list(scratch)

    def take(n):
        got = scratch[:n]
        del scratch[:n]
        return got

    rows_ref, routes_ref, router_ref = take(3)
    wg, wu, wd, acc, qbuf, kvbuf, sbuf, gathered, hid = take(9)
    sel, comb = take(3), take(3)
    pb, tx, rx, back, far, r2, s2, r1 = (take(len(PARTS)) for _ in range(8))
    send_sem, recv_sem, w_local, w_send, w_recv, kv_sem, q_sem, in_sem, info_send, info_recv = take(10)

    sec, dev = lax.axis_index("sec"), lax.axis_index("dev")
    pos = {"y": lax.div(dev, 16), "x": lax.rem(lax.div(dev, 4), 4), "z": lax.rem(dev, 4)}

    def peer(axis, k):
        other = lax.rem(pos[axis] + k, SIDE)
        return (sec, dev + (other - pos[axis]) * STRIDE[axis])

    mate = (1 - sec, dev)

    barrier = pltpu.get_barrier_semaphore()
    for axis in ("x", "y", "z"):
        for k in (1, 2, 3):
            pl.semaphore_signal(barrier, inc=1, device_id=peer(axis, k), device_id_type=MESH)
    pl.semaphore_signal(barrier, inc=1, device_id=mate, device_id_type=MESH)

    def kv_copy(i):
        slot = lax.rem(i, 2)
        return pltpu.make_async_copy(kv_hbm.at[i], kvbuf.at[slot], kv_sem.at[slot])

    small = [
        pltpu.make_async_copy(src, dst, in_sem.at[i])
        for i, (src, dst) in enumerate(((rows_hbm, rows_ref), (router_hbm, router_ref), (routes_hbm, routes_ref)))
    ]
    for copy in small:
        copy.start()
    q_copy = pltpu.make_async_copy(q_hbm, qbuf, q_sem)
    q_copy.start()
    kv_copy(0).start()
    w_pairs = ((wg_hbm, wg), (wu_hbm, wu), (wd_hbm, wd))
    local = [pltpu.make_async_copy(src.at[0], dst.at[sec], w_local.at[i]) for i, (src, dst) in enumerate(w_pairs)]

    def axes(p):
        return ROTATIONS[p % 3]

    def near(axis, k):
        return lax.rem(pos[axis] + k, SIDE)

    def copies(phase, p):
        a, b, c = axes(p)
        first, second = pl.ds(0, 2), pl.ds(2, 2)
        if phase == GATHER_A:
            src = pb[p].at[pos[b], pos[a], :, pl.ds(0, WIDTHS[p])]
            plan = [(a, k, src, src) for k in (2, 1, 3)]
        elif phase == GATHER_B:
            src = pb[p].at[pos[b]]
            plan = [(b, k, src, src) for k in (1, 3)]
        elif phase == RELAY_B:
            up, low = pb[p].at[near(b, 3), first], pb[p].at[near(b, 1), second]
            plan = [(b, 1, up, up), (b, 3, low, low)]
        elif phase == SPREAD:
            plan = [(c, k, tx[p].at[k - 1], rx[p].at[pos[c]]) for k in (2, 1, 3)]
        elif phase == RETURN:
            plan = [(c, k, rx[p].at[near(c, k)], back[p].at[3 - k]) for k in (2, 1, 3)]
        elif phase == FAR_B:
            cols = pl.ds(0, WIDTHS[p])
            plan = [
                (b, 1, pb[p].at[near(b, 2), first, :, cols], far[p].at[0]),
                (b, 3, pb[p].at[near(b, 2), second, :, cols], far[p].at[1]),
            ]
        elif phase == SUM_B:
            cols = pl.ds(0, WIDTHS[p])
            plan = [(b, k, pb[p].at[near(b, k), :, :, cols], r2[p].at[k // 2]) for k in (1, 3)]
        else:
            plan = [(a, k, s2[p].at[near(a, k)], r1[p].at[3 - k]) for k in (2, 1, 3)]
        return [
            pltpu.make_async_remote_copy(
                src_ref=src,
                dst_ref=dst,
                send_sem=send_sem.at[phase, p, i],
                recv_sem=recv_sem.at[phase, p, i],
                device_id=peer(axis, k),
                device_id_type=MESH,
            )
            for i, (axis, k, src, dst) in enumerate(plan)
        ]

    flights = {}

    def send(phase, p):
        flights[phase, p] = copies(phase, p)
        for copy in flights[phase, p]:
            copy.start()

    def arrived(phase, p):
        for copy in flights[phase, p]:
            copy.wait_recv()

    def sent(phase, p):
        for copy in flights[phase, p]:
            copy.wait_send()

    small[0].wait()
    for p in PARTS:
        a, b, _ = axes(p)
        pb[p][pos[b], pos[a], :, : WIDTHS[p]] = rows_ref[:, STARTS[p] : STARTS[p] + WIDTHS[p]]
    pl.semaphore_wait(barrier, 10)
    for p in FIRST:
        send(GATHER_A, p)
    for copy in small[1:]:
        copy.wait()

    affinity = jax.nn.sigmoid(dot_nt(router_ref[...], rows_ref[...]))
    hot = jnp.zeros((EXPERTS, TOK), F32)
    expert = iota((EXPERTS, TOK), 0)
    for k in range(SLOTS):
        hot = hot + jnp.where(routes_ref[k : k + 1, :] == expert, 1.0, 0.0)
    chosen = hot * affinity
    gates = ROUTE_SCALE * chosen / jnp.sum(chosen, axis=0, keepdims=True)
    earlier = jnp.where(iota((TOK, TOK), 0) < iota((TOK, TOK), 1), 1.0, 0.0).astype(BF)
    place = hot * (dot(hot.astype(BF), earlier) + 1.0)
    info = jnp.concatenate([place, gates], axis=0).T.astype(BF)

    info_flights = []
    for r in FIRST:
        a, b, _ = axes(r)
        mine = pb[r].at[pos[b], pos[a], :, pl.ds(WIDTHS[r], EXTRA)]
        mine[...] = info
        for k in (2, 1, 3):
            info_flights.append(
                pltpu.make_async_remote_copy(
                    src_ref=mine,
                    dst_ref=mine,
                    send_sem=info_send.at[r, k - 1],
                    recv_sem=info_recv.at[r, k - 1],
                    device_id=peer(a, k),
                    device_id_type=MESH,
                )
            )
    for copy in info_flights:
        copy.start()
    for p in PARTS[3:]:
        send(GATHER_A, p)
    kv_copy(1).start()
    for copy in local:
        copy.start()
    swaps = [
        pltpu.make_async_remote_copy(
            src_ref=src.at[0],
            dst_ref=dst.at[sec],
            send_sem=w_send.at[i],
            recv_sem=w_recv.at[i],
            device_id=mate,
            device_id_type=MESH,
        )
        for i, (src, dst) in enumerate(w_pairs)
    ]


    def attend(i):
        kv_copy(i).wait()
        keys = kvbuf.at[lax.rem(i, 2)]
        query = qbuf[i].T
        filled = len_ref[i]
        peak = jnp.full((128, 1), -1e30, F32)
        for j in range(4):
            s = dot(query, keys[:, j * 512 : (j + 1) * 512]) * SCORE_SCALE
            s = jnp.where(iota((128, 512), 1) + j * 512 < filled, s, -1e30)
            sbuf[:, j * 512 : (j + 1) * 512] = s
            peak = jnp.maximum(peak, jnp.max(s, axis=1, keepdims=True))
        total = jnp.zeros((128, 1), F32)
        out = jnp.zeros((128, LATENT), F32)
        for j in range(4):
            e = jnp.exp(sbuf[:, j * 512 : (j + 1) * 512] - peak)
            total = total + jnp.sum(e, axis=1, keepdims=True)
            out = out + dot_nt(e.astype(BF), keys[:LATENT, j * 512 : (j + 1) * 512])
        lat_ref[i] = (out / total).astype(BF)

    def lanes_of(r, shift):
        c = ROTATIONS[r][2]
        step = STRIDE[c]
        shape = (256, EXTRA)
        at = lax.rem(pos[c] + lax.div(iota(shape, 0), 64), SIDE)
        wanted = dev - pos[c] * step + at * step + shift
        return jnp.where(iota(shape, 1) == wanted, 1.0, 0.0).astype(BF)

    def info_of(r, half):
        w = WIDTHS[r]
        return pb[r][2 * half : 2 * half + 2, :, :, w : w + EXTRA].reshape(256, EXTRA)

    def build_sel(r):
        shape = (256, 256)
        row, col = iota(shape, 0), iota(shape, 1)
        same = lax.rem(lax.div(row, 8), 8) == lax.div(col, TOK)
        want = (lax.rem(row, 8) + 1).astype(F32)
        pick = lanes_of(r, 0)
        for half in range(2):
            got = dot_nt(pick, info_of(r, half))
            sel[r][half] = jnp.where(same & (got == want), 1.0, 0.0).astype(BF)

    def build_comb(r):
        shape = (256, 256)
        row, col = iota(shape, 0), iota(shape, 1)
        same = lax.rem(lax.div(col, 8), 8) == lax.div(row, TOK)
        want = (lax.rem(col, 8) + 1).astype(F32)
        pick, weigh = lanes_of(r, 0), lanes_of(r, EXPERTS)
        for half in range(2):
            got = dot_nt(info_of(r, half), pick)
            gate = dot_nt(info_of(r, half), weigh)
            comb[r][half] = jnp.where(same & (got == want), gate, 0.0).astype(BF)

    def spread(p):
        w, c = WIDTHS[p], axes(p)[2]
        for half in range(2):
            plane = pb[p][2 * half : 2 * half + 2, :, :, :w].reshape(256, w)
            got = dot(sel[p % 3][half], plane).astype(BF)
            at = slice(64 * half, 64 * half + 64)
            rx[p][pos[c], at] = got[:64]
            for j in range(1, SIDE):
                tx[p][j - 1, at] = got[64 * j : 64 * j + 64]

    def place_rows(p):
        w, r = WIDTHS[p], p % 3
        cols = slice(STARTS[p], STARTS[p] + w)
        if r == 1:
            gathered[:, cols] = rx[p][...].reshape(512, w)
            return
        source = {BLOCKS[r][i]: i for i in range(64)}
        loaded = {}

        def piece(block):
            i = source[block]
            if i // 2 not in loaded:
                at = 16 * ((i // 2) % 8)
                loaded[i // 2] = rx[p][i // 16, at : at + 16].astype(F32)
            return loaded[i // 2][8 * (i % 2) : 8 * (i % 2) + 8]

        for block in PLACING[r]:
            pair = jnp.concatenate([piece(block), piece(block + 1)], axis=0)
            gathered[8 * block : 8 * block + 16, cols] = pair.astype(BF)

    def gate_up(chunk):
        begin = STARTS[CHUNKS[chunk][0]]
        rows = slice(begin, begin + sum(WIDTHS[p] for p in CHUNKS[chunk]))

        @pl.loop(0, 2)
        def _(h):
            for n in range(2):
                cols = slice(256 * n, 256 * n + 256)
                parts = []
                for g, weight in enumerate((wg, wu)):
                    got = dot(gathered[:, rows], weight[h, rows, cols])
                    if chunk == 0:
                        acc[h, g, :, cols] = got
                    elif chunk < len(CHUNKS) - 1:
                        acc[h, g, :, cols] += got
                    else:
                        parts.append(got + acc[h, g, :, cols])
                if chunk == len(CHUNKS) - 1:
                    hid[h, :, cols] = (jax.nn.silu(parts[0]) * parts[1]).astype(BF)

    def down(p):
        w, r = WIDTHS[p], p % 3
        for n in range(0, w, 256):
            wide = min(256, w - n)
            cols = slice(STARTS[p] + n, STARTS[p] + n + wide)
            got = dot(hid[0], wd[0, :, cols]) + dot(hid[1], wd[1, :, cols])
            if r == 1:
                rx[p][:, :, n : n + wide] = got.astype(BF).reshape(SIDE, 128, wide)
                continue
            for i in range(0, 64, 2):
                one, two = BLOCKS[r][i], BLOCKS[r][i + 1]
                pair = jnp.concatenate([got[8 * one : 8 * one + 8], got[8 * two : 8 * two + 8]], axis=0)
                at = 8 * (i % 16)
                rx[p][i // 16, at : at + 16, n : n + wide] = pair.astype(BF)

    def combine(p):
        w, c = WIDTHS[p], axes(p)[2]
        for half in range(2):
            at = slice(64 * half, 64 * half + 64)
            got = jnp.concatenate([rx[p][pos[c], at]] + [back[p][j, at] for j in range(3)], axis=0)
            summed = dot(comb[p % 3][half], got).astype(BF)
            pb[p][2 * half : 2 * half + 2, :, :, :w] = summed.reshape(2, SIDE, TOK, w)

    def fold(p):
        w, b = WIDTHS[p], axes(p)[1]
        for k, half in ((1, 0), (3, 1)):
            at = (near(b, k), pl.ds(2 * half, 2), slice(None), pl.ds(0, w))
            pb[p][at] = (pb[p][at].astype(F32) + far[p][half].astype(F32)).astype(BF)

    def sum_b(p):
        w, b = WIDTHS[p], axes(p)[1]
        total = pb[p][pos[b], :, :, :w].astype(F32)
        for j in range(2):
            total = total + r2[p][j].astype(F32)
        s2[p][...] = total.astype(BF)

    def sum_a(p):
        a = axes(p)[0]
        total = s2[p][pos[a]].astype(F32)
        for j in range(3):
            total = total + r1[p][j].astype(F32)
        out_ref[:, STARTS[p] : STARTS[p] + WIDTHS[p]] = total.astype(BF)

    def begin_b(chunk):
        for p in CHUNKS[chunk]:
            arrived(GATHER_A, p)
            if chunk == 0:
                for copy in info_flights[3 * p : 3 * p + 3]:
                    copy.wait_recv()
            send(GATHER_B, p)

    def relay_b(chunk):
        for p in CHUNKS[chunk]:
            arrived(GATHER_B, p)
            send(RELAY_B, p)

    def begin_spread(chunk):
        for p in CHUNKS[chunk]:
            arrived(RELAY_B, p)
            if chunk == 0:
                build_sel(p)
            spread(p)
            send(SPREAD, p)

    def expert_in(chunk):
        for p in CHUNKS[chunk]:
            arrived(SPREAD, p)
            place_rows(p)
        gate_up(chunk)

    def expert_out(chunk):
        for p in CHUNKS[chunk]:
            down(p)
            send(RETURN, p)

    def begin_sum(chunk):
        for p in CHUNKS[chunk]:
            for phase in (GATHER_A, GATHER_B, RELAY_B):
                sent(phase, p)
            if p in FIRST:
                for copy in info_flights[3 * p : 3 * p + 3]:
                    copy.wait_send()
            arrived(RETURN, p)
            combine(p)
            send(FAR_B, p)

    def fold_b(chunk):
        for p in CHUNKS[chunk]:
            arrived(FAR_B, p)
            fold(p)
            send(SUM_B, p)

    def begin_a(chunk):
        for p in CHUNKS[chunk]:
            arrived(SUM_B, p)
            sum_b(p)
            send(SUM_A, p)

    def finish(chunk):
        for p in CHUNKS[chunk]:
            arrived(SUM_A, p)
            sum_a(p)

    q_copy.wait()
    attend(0)
    kv_copy(2).start()
    begin_b(0)
    begin_b(1)
    begin_b(2)
    for copy in swaps:
        copy.start()
    attend(1)
    kv_copy(3).start()
    attend(2)
    relay_b(0)
    relay_b(1)
    relay_b(2)
    attend(3)
    begin_spread(0)
    begin_spread(1)
    begin_spread(2)
    for r in range(3):
        build_comb(r)
    for i in range(2):
        local[i].wait()
        swaps[i].wait_recv()
    expert_in(0)
    expert_in(1)
    expert_in(2)
    local[2].wait()
    swaps[2].wait_recv()
    expert_out(0)
    expert_out(1)
    expert_out(2)
    begin_sum(0)
    begin_sum(1)
    begin_sum(2)
    fold_b(0)
    fold_b(1)
    fold_b(2)
    begin_a(0)
    begin_a(1)
    begin_a(2)
    finish(0)
    finish(1)
    finish(2)
    for copy in swaps:
        copy.wait_send()
    for phase in (SPREAD, RETURN, FAR_B, SUM_B, SUM_A):
        for p in PARTS:
            sent(phase, p)


def hand_over(lat_in, moe_in, lat_out, moe_out):
    lat_out[...] = lat_in[...]
    moe_out[...] = moe_in[...]


def per_device(queries, latent_cache, lengths, rows_in, routes, router_weight, gate_weight, up_weight, down_weight):
    queries, latent_cache = jnp.swapaxes(queries, 1, 2), jnp.swapaxes(latent_cache, 1, 2)
    routes, router_weight = routes.T, router_weight.T
    width = rows_in.shape[1]
    half = gate_weight.shape[2]
    vmem = pltpu.VMEM

    def each(make):
        return [make(p, WIDTHS[p]) for p in PARTS]

    scratch = [
        vmem(rows_in.shape, BF),
        vmem(routes.shape, jnp.int32),
        vmem(router_weight.shape, BF),
        vmem((2, width, half), BF),
        vmem((2, width, half), BF),
        vmem((2, half, width), BF),
        vmem((2, 2, 512, half), F32),
        vmem(queries.shape, BF),
        vmem((2,) + latent_cache.shape[1:], BF),
        vmem((queries.shape[2], latent_cache.shape[2]), F32),
    ]
    scratch += [vmem((512, width), BF), vmem((2, 512, half), BF)]
    scratch += [vmem((2, 256, 256), BF) for _ in range(6)]
    scratch += each(lambda p, w: vmem((SIDE, SIDE, TOK, w + (EXTRA if p in FIRST else 0)), BF))
    scratch += each(lambda p, w: vmem((3, 128, w), BF))
    scratch += each(lambda p, w: vmem((SIDE, 128, w), BF))
    scratch += each(lambda p, w: vmem((3, 128, w), BF))
    scratch += each(lambda p, w: vmem((2, 2, TOK, w), BF))
    scratch += each(lambda p, w: vmem((2, SIDE, TOK, w), BF))
    scratch += each(lambda p, w: vmem((SIDE, TOK, w), BF))
    scratch += each(lambda p, w: vmem((3, TOK, w), BF))
    dma = pltpu.SemaphoreType.DMA
    scratch += [dma((8, len(PARTS), 3)), dma((8, len(PARTS), 3)), dma((3,)), dma((3,)), dma((3,)), dma((2,)), dma]
    scratch += [dma((3,)), dma((3, 3)), dma((3, 3))]
    whole, stays = pl.BlockSpec(memory_space=pltpu.VMEM), pl.BlockSpec(memory_space=pl.ANY)
    results = pl.pallas_call(
        body,
        out_shape=(
            jax.ShapeDtypeStruct((queries.shape[0], queries.shape[2], LATENT), BF),
            jax.ShapeDtypeStruct(rows_in.shape, BF),
        ),
        in_specs=[pl.BlockSpec(memory_space=pltpu.SMEM)] + [stays] * 8,
        out_specs=(whole, whole),
        scratch_shapes=scratch,
        compiler_params=pltpu.CompilerParams(
            collective_id=0, has_side_effects=True, vmem_limit_bytes=63 << 20
        ),
    )(lengths, rows_in, routes, router_weight, queries, latent_cache, gate_weight, up_weight, down_weight)
    return pl.pallas_call(
        hand_over,
        out_shape=[jax.ShapeDtypeStruct(x.shape, x.dtype) for x in results],
        in_specs=[whole, whole],
        out_specs=[whole, whole],
        compiler_params=pltpu.CompilerParams(vmem_limit_bytes=63 << 20),
    )(*results)


def solution(mesh):
    return jax.shard_map(
        per_device,
        mesh=mesh,
        in_specs=(
            P(("sec", "dev"), None, None),
            P(("sec", "dev"), None, None),
            P(("sec", "dev")),
            P(("sec", "dev"), None),
            P(("sec", "dev"), None),
            P(),
            P("dev", None, "sec"),
            P("dev", None, "sec"),
            P("dev", "sec", None),
        ),
        out_specs=(P(("sec", "dev"), None, None), P(("sec", "dev"), None)),
        check_vma=False,
    )
```
